128 devices in a mesh: tier: 2 (over core), sub: 64 (over z, y, x).
Axes of the slice: x: 4, y: 4, z: 4, core: 2. Of those that a mesh axis runs over, the one named last changes fastest.
Arguments:
- ado_field: float32 [2, 96, 393216], P(None, None, ('tier', 'sub')), may hold values from -6 to 6
- hamiltonian: float32 [96, 96], replicated, may hold values from -0.625 to 0.625
- decay_rates: float32 [192], replicated, may hold values from 0.2 to 2
- bath_coef: float32 [2, 192], replicated, may hold values from -4 to 4
- counts: int32 [2, 64], P('tier', 'sub'), may hold values from 1 to 32, as said below
- child_slot: int32 [2, 32768], P('tier', 'sub'), may hold values from -1 to 31, as said below
- child_mode: int32 [2, 32768], P('tier', 'sub'), may hold values from 0 to 191, as said below
- child_occ: int32 [2, 32768], P('tier', 'sub'), may hold values from 1 to 3
- parent_slot: int32 [2, 32768], P('tier', 'sub'), may hold values from -1 to 31, as said below
- parent_mode: int32 [2, 32768], P('tier', 'sub'), may hold values from 0 to 191, as said below
Outputs:
- second_slope: float32 [2, 96, 393216], P(None, None, ('tier', 'sub'))
The draws below stay inside these ranges and needn't reach their ends.
Inputs may be any that keep to these rules, and one draw needn't show every extreme that they name: `counts`: some device of the last tier index and some device of the tier index before it are full with 32 live slots. `child_slot`: for each receiving sub index s2, the used positions q (entries >= 0, each a live slot of the device) come first among the 8 positions, followed by -1. No used position at tier index 0. In every draw some device receives 8 used positions from every sub index of the band above. `child_mode`: the mode of each position, used or not. `parent_slot`: entry (t, s2 * 64 * 8 + s * 8 + q) is a live slot of device (t, s2) exactly where child_slot[t + 1, s * 64 * 8 + s2 * 8 + q] >= 0, else -1; -1 throughout at the last tier index. `parent_mode`: equal to the child's mode at the same edge; zero at the last tier index.
All inputs are finite; a program needn't handle non-finite values.
Results may differ from the reference program's by a relative error of at most 0.0003.
Values sent between devices are 32-bit elements; how exact they have to be, the bound alone decides.
A program may use at most 64 MiB of HBM per device.

```python
import math
import jax
import jax.numpy as jnp
from jax import lax

D = 96
MODES = 192
ADO_DEV = 32
ADOS = 4096
N_TIER = 2
N_SUB = 64


def edge_plan(key):
    key_list = jax.random.split(key, 10)
    slot_cap = 16 * ADO_DEV // N_SUB
    tier_rank = jnp.arange(N_TIER)[:, None]
    base_count = ADO_DEV // 4 + 3 * ADO_DEV // 4 * (tier_rank + 1) // N_TIER
    shortfall = jax.random.randint(key_list[0], (N_TIER, N_SUB), 0, max(ADO_DEV // 8, 2))
    live_count = jnp.maximum(base_count - shortfall, 1)
    full_sub = jax.random.randint(key_list[1], (), 0, N_SUB)
    parent_sub = jax.random.randint(key_list[9], (), 0, N_SUB)
    live_count = live_count.at[N_TIER - 1, full_sub].set(ADO_DEV)
    live_count = live_count.at[N_TIER - 2, parent_sub].set(ADO_DEV)
    fill_level = jax.random.randint(key_list[2], (N_TIER, N_SUB, N_SUB), slot_cap // 4, slot_cap + 1)
    full_tier = jax.random.randint(key_list[3], (), 1, N_TIER)
    busy_sub = jax.random.randint(key_list[4], (), 0, N_SUB)
    fill_level = fill_level.at[full_tier, :, busy_sub].set(slot_cap)
    fill_level = fill_level.at[0].set(0)
    fill_level = fill_level.at[N_TIER - 1, full_sub, parent_sub].set(jnp.maximum(fill_level[N_TIER - 1, full_sub, parent_sub], 1))
    edge_shape = (N_TIER, N_SUB, N_SUB, slot_cap)
    position = jnp.arange(slot_cap)[None, None, None, :]
    used_slot = position < fill_level[:, :, :, None]
    own_slot = jax.random.randint(key_list[5], edge_shape, 0, live_count[:, :, None, None])
    own_slot = own_slot.at[N_TIER - 1, full_sub, parent_sub, 0].set(ADO_DEV - 1)
    below_count = jnp.concatenate([jnp.ones((1, N_SUB), live_count.dtype), live_count[:-1]], axis=0)
    far_slot = jax.random.randint(key_list[6], edge_shape, 0, below_count[:, None, :, None])
    far_slot = far_slot.at[N_TIER - 1, full_sub, parent_sub, 0].set(ADO_DEV - 1)
    mode_index = jax.random.randint(key_list[7], edge_shape, 0, MODES)
    occupancy = jax.random.randint(key_list[8], edge_shape, 1, 4)
    child_list = jnp.where(used_slot, own_slot, -1)
    far_slot = jnp.where(used_slot, far_slot, -1)
    turned_slot = jnp.transpose(far_slot, (0, 2, 1, 3))
    turned_mode = jnp.transpose(mode_index, (0, 2, 1, 3))
    parent_list = jnp.concatenate([turned_slot[1:], -jnp.ones_like(turned_slot[:1])], axis=0)
    parent_modes = jnp.concatenate([turned_mode[1:], jnp.zeros_like(turned_mode[:1])], axis=0)
    flat_shape = (N_TIER, N_SUB * N_SUB * slot_cap)
    return (live_count.astype(jnp.int32), child_list.reshape(flat_shape).astype(jnp.int32), mode_index.reshape(flat_shape).astype(jnp.int32), occupancy.reshape(flat_shape).astype(jnp.int32), parent_list.reshape(flat_shape).astype(jnp.int32), parent_modes.reshape(flat_shape).astype(jnp.int32))


def draw_counts(key, part):
    return edge_plan(key)[0]


def draw_child_slot(key, part):
    return edge_plan(key)[1]


def draw_child_mode(key, part):
    return edge_plan(key)[2]


def draw_child_occ(key, part):
    return edge_plan(key)[3]


def draw_parent_slot(key, part):
    return edge_plan(key)[4]


def draw_parent_mode(key, part):
    return edge_plan(key)[5]


def level_of(stream_key, dims, pieces, low, top_value):
    def one(dim, blocks):
        steps = jax.random.uniform(jax.random.fold_in(jax.random.fold_in(stream_key, 6), dim), (blocks,), jnp.float32, low / len(pieces), top_value / len(pieces))
        return jnp.repeat(jnp.exp(steps), dims[dim] // blocks).reshape((-1,) + (1,) * (len(dims) - dim - 1))

    gain = one(*pieces[0])
    for cut in pieces[1:]:
        gain = gain * one(*cut)
    return gain


def bell_draw(key, extent, deviation, most, cuts=(), kind=jnp.bfloat16):
    factor_of = level_of(key, extent, cuts, -0.22, 0.18) if cuts else 1.0
    result = jax.random.normal(key, extent, jnp.float32) * deviation * factor_of
    return jnp.minimum(jnp.maximum(result, -most), most).astype(kind)


def setup_inputs(seed: int = 0) -> dict:
    key_of = jax.random.split(jax.random.key(seed), 11)
    return {
        "ado_field": bell_draw(key_of[0], (2, D, ADOS * D), 1.0, 6.0, ((2, 128),), jnp.float32),
        "hamiltonian": bell_draw(key_of[1], (D, D), D ** -0.5, 0.625, (), jnp.float32),
        "decay_rates": jnp.clip(jnp.exp(jax.random.uniform(key_of[2], (MODES,), jnp.float32, math.log(0.2), math.log(2.0))), 0.2, 2.0),
        "bath_coef": bell_draw(key_of[3], (2, MODES), 1.0, 4.0, (), jnp.float32),
        "counts": draw_counts(jax.random.fold_in(key_of[10], 71), 0),
        "child_slot": draw_child_slot(jax.random.fold_in(key_of[10], 71), 0),
        "child_mode": draw_child_mode(jax.random.fold_in(key_of[10], 71), 0),
        "child_occ": draw_child_occ(jax.random.fold_in(key_of[10], 71), 0),
        "parent_slot": draw_parent_slot(jax.random.fold_in(key_of[10], 71), 0),
        "parent_mode": draw_parent_mode(jax.random.fold_in(key_of[10], 71), 0),
    }


step_size = 0.2


def gather_strips(stacked, owner_index, slot_list, mode_list):
    validity = slot_list >= 0
    slot_index = jnp.where(validity, slot_list, 0)
    site_index = mode_list // 2
    row_part = stacked[owner_index, :, site_index, slot_index, :]
    col_part = stacked[owner_index, :, :, slot_index, site_index]
    packed = jnp.concatenate([row_part, col_part], axis=-2)
    return packed * validity[..., None, None].astype(jnp.float32)


def local_slope(packed, hamilton, decay_rates, bath_coef):
    state_grid, from_children, from_parents, child_slot, child_mode, child_occ, parent_slot, parent_mode = packed
    left_product = jnp.einsum("ij,pjck->pick", hamilton, state_grid, precision=lax.Precision.HIGHEST)
    right_product = jnp.einsum("picj,jk->pick", state_grid, hamilton, precision=lax.Precision.HIGHEST)
    slope_field = jnp.stack([left_product[1] - right_product[1], right_product[0] - left_product[0]])
    child_valid = child_slot >= 0
    child_index = jnp.where(child_valid, child_slot, 0)
    child_site = child_mode // 2
    weight = jnp.where(child_valid, child_occ, 0).astype(jnp.float32)
    decay_rate = jnp.zeros((state_grid.shape[2],), jnp.float32).at[child_index].add(weight * decay_rates[child_mode])
    slope_field = slope_field - decay_rate[None, None, :, None] * state_grid
    parent_valid = parent_slot >= 0
    parent_index = jnp.where(parent_valid, parent_slot, 0)
    parent_site = parent_mode // 2
    received = from_children * parent_valid[:, None, None].astype(jnp.float32)
    row_add = jnp.stack([received[:, 1], -received[:, 0]])
    col_add = jnp.transpose(jnp.stack([-received[:, 3], received[:, 2]]), (0, 2, 1))
    slope_field = slope_field.at[:, parent_site, parent_index, :].add(row_add)
    slope_field = slope_field.at[:, :, parent_index, parent_site].add(col_add)
    real_coef = (bath_coef[0][child_mode] * weight)[:, None]
    imag_coef = (bath_coef[1][child_mode] * weight)[:, None]
    row_re, row_im, col_re, col_im = from_parents[:, 0], from_parents[:, 1], from_parents[:, 2], from_parents[:, 3]
    row_add = jnp.stack([real_coef * row_im + imag_coef * row_re, imag_coef * row_im - real_coef * row_re])
    col_add = jnp.stack([imag_coef * col_re - real_coef * col_im, real_coef * col_re + imag_coef * col_im])
    slope_field = slope_field.at[:, child_site, child_index, :].add(row_add)
    slope_field = slope_field.at[:, :, child_index, child_site].add(jnp.transpose(col_add, (0, 2, 1)))
    return slope_field


def reference(ado_field, hamiltonian, decay_rates, bath_coef, counts, child_slot, child_mode, child_occ, parent_slot, parent_mode):
    devices_all = N_TIER * N_SUB
    slot_cap = 16 * ADO_DEV // N_SUB
    edge_shape = (N_TIER, N_SUB, N_SUB, slot_cap)
    hamilton = 0.5 * (hamiltonian + hamiltonian.T)
    stacked = jnp.transpose(ado_field.reshape(2, D, devices_all, ADO_DEV, D), (2, 0, 1, 3, 4))
    live_mask = (jnp.arange(ADO_DEV)[None, :] < counts.reshape(devices_all, 1)).astype(jnp.float32)
    stacked = stacked * live_mask[:, None, None, :, None]
    owner_index = jnp.arange(N_TIER)[:, None, None, None] * N_SUB + jnp.arange(N_SUB)[None, :, None, None]
    child_edges = (child_slot.reshape(edge_shape), child_mode.reshape(edge_shape))
    parent_edges = (parent_slot.reshape(edge_shape), parent_mode.reshape(edge_shape))
    per_device = (child_slot.reshape(devices_all, -1), child_mode.reshape(devices_all, -1), child_occ.reshape(devices_all, -1), parent_slot.reshape(devices_all, -1), parent_mode.reshape(devices_all, -1))

    def coupled_strips(ensemble):
        downward = jnp.swapaxes(gather_strips(ensemble, owner_index, child_edges[0], child_edges[1]), 1, 2)
        upward = jnp.swapaxes(gather_strips(ensemble, owner_index, parent_edges[0], parent_edges[1]), 1, 2)
        from_children = jnp.concatenate([downward[1:], jnp.zeros_like(downward[:1])], axis=0)
        from_parents = jnp.concatenate([jnp.zeros_like(upward[:1]), upward[:-1]], axis=0)
        return from_children.reshape(devices_all, N_SUB * slot_cap, 4, D), from_parents.reshape(devices_all, N_SUB * slot_cap, 4, D)

    from_children, from_parents = coupled_strips(stacked)
    second_state = lax.map(lambda packed: packed[0] + 0.5 * step_size * local_slope(packed, hamilton, decay_rates, bath_coef), (stacked, from_children, from_parents, per_device[0], per_device[1], per_device[2], per_device[3], per_device[4]))
    from_children, from_parents = coupled_strips(second_state)
    slopes = lax.map(lambda packed: local_slope(packed, hamilton, decay_rates, bath_coef), (second_state, from_children, from_parents, per_device[0], per_device[1], per_device[2], per_device[3], per_device[4]))
    return jnp.transpose(slopes, (1, 2, 0, 3, 4)).reshape(2, D, devices_all * ADO_DEV * D)
```

```python
import functools

import jax
import jax.numpy as jnp
from jax import lax
from jax.experimental import pallas as pl
from jax.experimental.pallas import tpu as pltpu
from jax.sharding import PartitionSpec as P

MESH = pl.DeviceIdType.MESH
D = 96
SLOTS = 32
SUBS = 64
CAP = 8
EDGES = SUBS * CAP
ROWS = SLOTS * D
GROUP = 4
WIDE = GROUP * D
GROUPS = SLOTS // GROUP
HALF_STEP = 0.1
F32 = jnp.float32
BF16 = jnp.bfloat16


def hops(offset):
    return sum((0, 1, 2, 1)[d] for d in (offset // 16, offset // 4 % 4, offset % 4))


def partner_order():
    seen, groups = set(), []
    for c in range(SUBS):
        v, group = (c // 16, c // 4 % 4, c % 4), []
        for r in range(3):
            for sign in (1, -1):
                u = tuple(sign * v[(r + k) % 3] % 4 for k in range(3))
                if u not in seen:
                    seen.add(u)
                    group.append(u[0] * 16 + u[1] * 4 + u[2])
        if group:
            groups.append(group)
    groups.sort(key=lambda g: -hops(g[0]))
    return [o for g in groups for o in g]


ORDER = partner_order()


def partner(me, offset, sign):
    dz, dy, dx = offset // 16, offset // 4 % 4, offset % 4
    if sign < 0:
        dz, dy, dx = (4 - dz) % 4, (4 - dy) % 4, (4 - dx) % 4
    z, y, x = me // 16, me // 4 % 4, me % 4
    return (z + dz) % 4 * 16 + (y + dy) % 4 * 4 + (x + dx) % 4


def split(value):
    high = value.astype(BF16)
    return high, (value - high.astype(F32)).astype(BF16)


def mm(a, b):
    return jnp.dot(a, b, preferred_element_type=F32)


def roll(value, shift):
    return pltpu.roll(value, shift, 1)


def lanes(shape):
    return lax.broadcasted_iota(jnp.int32, shape, len(shape) - 1)


def turn(value):
    return jnp.concatenate([value, jnp.zeros((128 - D, 128), F32)], axis=0).T


def kernel(
    x_hbm, h_hbm, rate_hbm, coef_hbm, count_hbm, cslot_hbm, cmode_hbm, cocc_hbm, pslot_hbm, pmode_hbm,
    out_hbm,
    x_v, h_v, rate_v, coef_v, lists_v, row_v, count_s, row_s,
    state, acc, hot, v_hi, v_lo, strips, send, recv, coef_t, decay, out_v,
    in_sem, small_sem, out_sem, send_sem, recv_sem,
):
    tier, me = lax.axis_index("tier"), lax.axis_index("sub")
    other = 1 - tier
    barrier = pltpu.get_barrier_semaphore()
    for o in ORDER:
        pl.semaphore_signal(barrier, 1, device_id=(other, partner(me, o, 1)), device_id_type=MESH)

    smalls = [
        pltpu.make_async_copy(cslot_hbm, lists_v.at[0], small_sem.at[0]),
        pltpu.make_async_copy(pslot_hbm, lists_v.at[1], small_sem.at[1]),
        pltpu.make_async_copy(cmode_hbm, lists_v.at[2], small_sem.at[2]),
        pltpu.make_async_copy(pmode_hbm, lists_v.at[3], small_sem.at[3]),
        pltpu.make_async_copy(cocc_hbm, lists_v.at[4], small_sem.at[4]),
        pltpu.make_async_copy(count_hbm, count_s, small_sem.at[5]),
        pltpu.make_async_copy(h_hbm, h_v, small_sem.at[6]),
        pltpu.make_async_copy(rate_hbm, rate_v, small_sem.at[7]),
        pltpu.make_async_copy(coef_hbm, coef_v, small_sem.at[8]),
    ]
    for copy in smalls:
        copy.start()

    def x_copy(g):
        at = pl.ds(pl.multiple_of(g * WIDE, 128), WIDE)
        return pltpu.make_async_copy(x_hbm.at[:, :, at], x_v.at[:, :, at], in_sem.at[g])

    for g in range(GROUPS):
        x_copy(g).start()
    for copy in smalls:
        copy.wait()

    below = tier == 0
    slot = jnp.where(below, lists_v[1], lists_v[0])
    mode = jnp.where(below, lists_v[3], lists_v[2])
    row_v[...] = jnp.where(slot >= 0, slot * D + mode // 2, 0)
    to_scalars = pltpu.make_async_copy(row_v, row_s, small_sem.at[0])
    to_scalars.start()

    count = count_s[0, 0]

    def load(g, carry):
        x_copy(g).wait()
        at = pl.ds(pl.multiple_of(g * WIDE, 128), WIDE)
        live = lanes((D, WIDE)) // D + g * GROUP < count
        lane = lanes((D, 128))
        for p in range(2):
            x = jnp.where(live, x_v[p, :, at], 0.0)
            t0, t1, t2 = x[:, :128], x[:, 128:256], x[:, 256:]
            parts = (
                t0,
                jnp.where(lane < 32, roll(t0, 32), roll(t1, 32)),
                jnp.where(lane < 64, roll(t1, 64), roll(t2, 64)),
                roll(t2, 96),
            )
            for j, part in enumerate(parts):
                state[p, pl.ds(pl.multiple_of(g * WIDE + j * D, 8), D), :] = part
            for j, part in enumerate((t0, t1, t2)):
                state[2 + p, pl.ds(pl.multiple_of(g * WIDE + j * 128, 8), 128), :] = turn(part)
        return carry

    lax.fori_loop(0, GROUPS, load, 0)
    to_scalars.wait()
    pl.semaphore_wait(barrier, SUBS)

    def remote(s, i):
        return pltpu.make_async_remote_copy(
            send.at[s, pl.ds(i * CAP, CAP)],
            recv.at[s, pl.ds(i * CAP, CAP)],
            send_sem.at[s, i],
            recv_sem.at[s, i],
            device_id=(other, partner(me, ORDER[i], 1)),
            device_id_type=MESH,
        )

    def send_strips(s):
        lane = lanes((CAP, 128))
        for i, o in enumerate(ORDER):
            first = partner(me, o, 1) * CAP
            for k in range(CAP):
                r = row_s[0, first + k]
                for p in range(4):
                    strips[p, pl.ds(i * CAP + k, 1), :] = state[p, pl.ds(r, 1), :]
            at = pl.ds(i * CAP, CAP)
            a, b, c, d = (strips[p, at, :] for p in range(4))
            b, c = roll(b, 96), roll(c, 64)
            send[s, at, 0:128] = jnp.where(lane < D, a, b)
            send[s, at, 128:256] = jnp.where(lane < 64, b, c)
            send[s, at, 256:384] = jnp.where(lane < 32, c, roll(d, 32))
            remote(s, i).start()

    send_strips(0)

    sub_lane = lanes((1, EDGES))
    offset = jnp.zeros((1, EDGES), jnp.int32)
    for i, o in enumerate(ORDER):
        offset = jnp.where(sub_lane // CAP == i, o, offset)
    z = (me // 16 + 4 - offset // 16) % 4
    y = (me // 4 + 4 - offset // 4 % 4) % 4
    x = (me + 4 - offset % 4) % 4
    source = (z * 16 + y * 4 + x) * CAP + sub_lane % CAP
    order = jnp.where(lax.broadcasted_iota(jnp.int32, (EDGES, EDGES), 0) == source, 1.0, 0.0).astype(BF16)
    listed = jnp.concatenate(
        [slot.astype(F32), mode.astype(F32), lists_v[4].astype(F32), jnp.zeros((13, EDGES), F32)], axis=0
    )
    listed = mm(listed.astype(BF16), order)
    slot = listed[0:1].astype(jnp.int32)
    mode = listed[1:2].astype(jnp.int32)
    weight = jnp.where(slot >= 0, listed[2:3], 0.0)
    modes = rate_v.shape[1]
    table = jnp.concatenate([rate_v[...], coef_v[...], jnp.zeros((5, modes), F32)], axis=0)
    high, rest = split(table)
    middle, low = split(table - high.astype(F32))
    is_mode = jnp.where(lax.broadcasted_iota(jnp.int32, (modes, EDGES), 0) == mode, 1.0, 0.0).astype(BF16)
    pieces = mm(jnp.concatenate([high.astype(F32), middle.astype(F32), low.astype(F32), jnp.zeros((8, modes), F32)], axis=0).astype(BF16), is_mode)
    per_edge = pieces[0:8] + pieces[8:16] + pieces[16:24]
    one = jnp.where(slot >= 0, 1.0, 0.0)
    loss = jnp.where(below, 0.0, weight * per_edge[0:1])
    c_re = jnp.where(below, one, weight * per_edge[1:2])
    c_im = jnp.where(below, 0.0, weight * per_edge[2:3])
    of_slot = lax.broadcasted_iota(jnp.int32, (SLOTS, EDGES), 0) == slot
    total = jnp.sum(jnp.where(of_slot, loss, 0.0), axis=1, keepdims=True)
    decay[...] = jnp.broadcast_to(total, (SLOTS, 128))
    columns = jnp.concatenate([c_re, c_im, jnp.zeros((126, EDGES), F32)], axis=0)
    for j in range(EDGES // 128):
        coef_t[j * 128 : (j + 1) * 128, :] = columns[:, j * 128 : (j + 1) * 128].T
    target = jnp.where(slot >= 0, slot * D + mode // 2, -1)

    def mark(g, carry):
        at = pl.multiple_of(g * WIDE, 128)
        row = lax.broadcasted_iota(jnp.int32, (WIDE, EDGES), 0) + at
        hot[pl.ds(at, WIDE), :] = jnp.where(row == target, 1.0, 0.0).astype(BF16)
        return carry

    lax.fori_loop(0, GROUPS, mark, 0)
    h = 0.5 * (h_v[...] + h_v[...].T)
    h_hi, h_lo = split(h)

    def products(c, carry):
        at = pl.ds(pl.multiple_of(c * D, 8), D)
        q_hi, q_lo = split(jnp.concatenate([state[p, at, :] for p in range(4)], axis=1))
        r = mm(h_hi, q_hi) + (mm(h_hi, q_lo) + mm(h_lo, q_hi))
        acc[0, at, :] = r[:, 128:256]
        acc[1, at, :] = -r[:, 0:128]
        acc[2, at, :] = -r[:, 384:512]
        acc[3, at, :] = r[:, 256:384]
        return carry

    def receive(s):
        lane = lanes((2 * CAP, 128))
        for i in range(SUBS):
            remote(s, i).wait_recv()
            if i % 2:
                at = pl.ds((i - 1) * CAP, 2 * CAP)
                t0, t1, t2 = (recv[s, at, q * 128 : (q + 1) * 128] for q in range(3))
                a = t0
                b = jnp.where(lane < 32, roll(t0, 32), roll(t1, 32))
                c = jnp.where(lane < 64, roll(t1, 64), roll(t2, 64))
                d = roll(t2, 96)
                c_re, c_im = coef_t[at, 0:1], coef_t[at, 1:2]
                v = jnp.concatenate(
                    [c_im * a + c_re * b, c_im * b - c_re * a, c_im * c - c_re * d, c_im * d + c_re * c], axis=1
                )
                v_hi[at, :], v_lo[at, :] = split(v)

    def combine(g, carry, last):
        base = pl.multiple_of(g * WIDE, 128)
        marks = hot[pl.ds(base, WIDE), :]
        added = mm(marks, v_hi[...]) + mm(marks, v_lo[...])
        results = []
        for j in range(GROUP):
            at = pl.ds(pl.multiple_of(base + j * D, 8), D)
            a_re, a_im, b_re, b_im = (
                acc[p, at, :] + added[j * D : (j + 1) * D, p * 128 : (p + 1) * 128] for p in range(4)
            )
            rate = decay[pl.ds(g * GROUP + j, 1), :]
            x_re, x_im = state[0, at, :], state[1, at, :]
            s_re = a_re + turn(b_re)[:D] - rate * x_re
            s_im = a_im + turn(b_im)[:D] - rate * x_im
            if last:
                results.append((s_re, s_im))
            else:
                y_re, y_im = state[2, at, :], state[3, at, :]
                state[0, at, :] = x_re + HALF_STEP * s_re
                state[1, at, :] = x_im + HALF_STEP * s_im
                state[2, at, :] = y_re + HALF_STEP * (turn(a_re)[:D] + b_re - rate * y_re)
                state[3, at, :] = y_im + HALF_STEP * (turn(a_im)[:D] + b_im - rate * y_im)
        if last:
            lane = lanes((D, 128))
            at = pl.ds(base, WIDE)
            for p in range(2):
                s0, s1, s2, s3 = (r[p] for r in results)
                s1, s2 = roll(s1, 96), roll(s2, 64)
                out_v[p, :, pl.ds(base, 128)] = jnp.where(lane < D, s0, s1)
                out_v[p, :, pl.ds(pl.multiple_of(base + 128, 128), 128)] = jnp.where(lane < 64, s1, s2)
                out_v[p, :, pl.ds(pl.multiple_of(base + 256, 128), 128)] = jnp.where(lane < 32, s2, roll(s3, 32))
            out_copy(g).start()
        return carry

    def out_copy(g):
        at = pl.ds(pl.multiple_of(g * WIDE, 128), WIDE)
        return pltpu.make_async_copy(out_v.at[:, :, at], out_hbm.at[:, :, at], out_sem.at[g])

    lax.fori_loop(0, SLOTS, products, 0)
    receive(0)
    lax.fori_loop(0, GROUPS, functools.partial(combine, last=False), 0)
    send_strips(1)
    lax.fori_loop(0, SLOTS, products, 0)
    receive(1)
    lax.fori_loop(0, GROUPS, functools.partial(combine, last=True), 0)
    for s in range(2):
        for i in range(SUBS):
            remote(s, i).wait_send()
    for g in range(GROUPS):
        out_copy(g).wait()


def on_device(ado_field, hamiltonian, decay_rates, bath_coef, counts, child_slot, child_mode, child_occ, parent_slot, parent_mode):
    modes = decay_rates.shape[0]
    scratch = [
        pltpu.VMEM((2, D, ROWS), F32),
        pltpu.VMEM((D, D), F32),
        pltpu.VMEM((1, modes), F32),
        pltpu.VMEM((2, modes), F32),
        pltpu.VMEM((5, 1, EDGES), jnp.int32),
        pltpu.VMEM((1, EDGES), jnp.int32),
        pltpu.SMEM((1, 1), jnp.int32),
        pltpu.SMEM((1, EDGES), jnp.int32),
        pltpu.VMEM((4, ROWS, 128), F32),
        pltpu.VMEM((4, ROWS, 128), F32),
        pltpu.VMEM((ROWS, EDGES), BF16),
        pltpu.VMEM((EDGES, 512), BF16),
        pltpu.VMEM((EDGES, 512), BF16),
        pltpu.VMEM((4, EDGES, 128), F32),
        pltpu.VMEM((2, EDGES, WIDE), F32),
        pltpu.VMEM((2, EDGES, WIDE), F32),
        pltpu.VMEM((EDGES, 128), F32),
        pltpu.VMEM((SLOTS, 128), F32),
        pltpu.VMEM((2, D, ROWS), F32),
        pltpu.SemaphoreType.DMA((GROUPS,)),
        pltpu.SemaphoreType.DMA((9,)),
        pltpu.SemaphoreType.DMA((GROUPS,)),
        pltpu.SemaphoreType.DMA((2, SUBS)),
        pltpu.SemaphoreType.DMA((2, SUBS)),
    ]
    return pl.pallas_call(
        kernel,
        out_shape=jax.ShapeDtypeStruct((2, D, ROWS), F32),
        in_specs=[pl.BlockSpec(memory_space=pl.ANY)] * 10,
        out_specs=pl.BlockSpec(memory_space=pl.ANY),
        scratch_shapes=scratch,
        compiler_params=pltpu.CompilerParams(collective_id=0, has_side_effects=True, vmem_limit_bytes=48 << 20),
        cost_estimate=pl.CostEstimate(flops=10**10, bytes_accessed=5 * 10**6, transcendentals=0),
    )(
        ado_field, hamiltonian, decay_rates.reshape(1, modes), bath_coef, counts,
        child_slot, child_mode, child_occ, parent_slot, parent_mode,
    )


def solution(mesh):
    edges = P("tier", "sub")
    return jax.shard_map(
        on_device,
        mesh=mesh,
        in_specs=(P(None, None, ("tier", "sub")), P(), P(), P(), edges, edges, edges, edges, edges, edges),
        out_specs=P(None, None, ("tier", "sub")),
        check_vma=False,
    )
```

```python
import functools

import jax
import jax.numpy as jnp
from jax import lax
from jax.experimental import pallas as pl
from jax.experimental.pallas import tpu as pltpu
from jax.sharding import PartitionSpec as P

MESH = pl.DeviceIdType.MESH
D = 96
SLOTS = 32
SUBS = 64
CAP = 8
EDGES = SUBS * CAP
ROWS = SLOTS * D
GROUP = 4
WIDE = GROUP * D
GROUPS = SLOTS // GROUP
CHUNKS = EDGES // 128
EARLY = 1
HALF_STEP = 0.1
F32 = jnp.float32
BF16 = jnp.bfloat16


def hops(offset):
    return sum((0, 1, 2, 1)[d] for d in (offset // 16, offset // 4 % 4, offset % 4))


def partner_order():
    seen, groups = set(), []
    for c in range(SUBS):
        v, group = (c // 16, c // 4 % 4, c % 4), []
        for r in range(3):
            for sign in (1, -1):
                u = tuple(sign * v[(r + k) % 3] % 4 for k in range(3))
                if u not in seen:
                    seen.add(u)
                    group.append(u[0] * 16 + u[1] * 4 + u[2])
        if group:
            groups.append(group)
    groups.sort(key=lambda g: -hops(g[0]))
    return [o for g in groups for o in g]


ORDER = partner_order()


def partner(me, offset, sign):
    dz, dy, dx = offset // 16, offset // 4 % 4, offset % 4
    if sign < 0:
        dz, dy, dx = (4 - dz) % 4, (4 - dy) % 4, (4 - dx) % 4
    z, y, x = me // 16, me // 4 % 4, me % 4
    return (z + dz) % 4 * 16 + (y + dy) % 4 * 4 + (x + dx) % 4


def split(value):
    high = value.astype(BF16)
    return high, (value - high.astype(F32)).astype(BF16)


def mm(a, b):
    return jnp.dot(a, b, preferred_element_type=F32)


def roll(value, shift):
    return pltpu.roll(value, shift, 1)


def lanes(shape):
    return lax.broadcasted_iota(jnp.int32, shape, len(shape) - 1)


def turn(value):
    return jnp.concatenate([value, jnp.zeros((128 - D, 128), F32)], axis=0).T


def kernel(
    x_hbm, h_hbm, rate_hbm, coef_hbm, count_hbm, cslot_hbm, cmode_hbm, cocc_hbm, pslot_hbm, pmode_hbm,
    out_v,
    x_v, h_v, rate_v, coef_v, lists_v, row_v, count_s, row_s,
    state, acc, hot, v_both, factor, strips, send, recv, coef_t, decay,
    in_sem, small_sem, send_sem, recv_sem,
):
    tier, me = lax.axis_index("tier"), lax.axis_index("sub")
    other = 1 - tier
    barrier = pltpu.get_barrier_semaphore()
    for o in ORDER:
        pl.semaphore_signal(barrier, 1, device_id=(other, partner(me, o, 1)), device_id_type=MESH)

    smalls = [
        pltpu.make_async_copy(cslot_hbm, lists_v.at[0], small_sem.at[0]),
        pltpu.make_async_copy(pslot_hbm, lists_v.at[1], small_sem.at[1]),
        pltpu.make_async_copy(cmode_hbm, lists_v.at[2], small_sem.at[2]),
        pltpu.make_async_copy(pmode_hbm, lists_v.at[3], small_sem.at[3]),
        pltpu.make_async_copy(cocc_hbm, lists_v.at[4], small_sem.at[4]),
        pltpu.make_async_copy(count_hbm, count_s, small_sem.at[5]),
        pltpu.make_async_copy(h_hbm, h_v, small_sem.at[6]),
        pltpu.make_async_copy(rate_hbm, rate_v, small_sem.at[7]),
        pltpu.make_async_copy(coef_hbm, coef_v, small_sem.at[8]),
    ]
    for copy in smalls:
        copy.start()

    def x_copy(g):
        at = pl.ds(pl.multiple_of(g * WIDE, 128), WIDE)
        return pltpu.make_async_copy(x_hbm.at[:, :, at], x_v.at[:, :, at], in_sem.at[g])

    for g in range(GROUPS):
        x_copy(g).start()
    for copy in smalls:
        copy.wait()

    below = tier == 0
    slot = jnp.where(below, lists_v[1], lists_v[0])
    mode = jnp.where(below, lists_v[3], lists_v[2])
    row_v[...] = jnp.where(slot >= 0, slot * D + mode // 2, 0)
    to_scalars = pltpu.make_async_copy(row_v, row_s, small_sem.at[0])
    to_scalars.start()

    count = count_s[0, 0]

    def load(g, carry):
        x_copy(g).wait()
        at = pl.ds(pl.multiple_of(g * WIDE, 128), WIDE)
        live = lanes((D, WIDE)) // D + g * GROUP < count
        lane = lanes((D, 128))
        for p in range(2):
            x = jnp.where(live, x_v[p, :, at], 0.0)
            t0, t1, t2 = x[:, :128], x[:, 128:256], x[:, 256:]
            parts = (
                t0,
                jnp.where(lane < 32, roll(t0, 32), roll(t1, 32)),
                jnp.where(lane < 64, roll(t1, 64), roll(t2, 64)),
                roll(t2, 96),
            )
            for j, part in enumerate(parts):
                state[p, pl.ds(pl.multiple_of(g * WIDE + j * D, 8), D), :] = part
            for j, part in enumerate((t0, t1, t2)):
                state[2 + p, pl.ds(pl.multiple_of(g * WIDE + j * 128, 8), 128), :] = turn(part)
        return carry

    lax.fori_loop(0, GROUPS, load, 0)
    to_scalars.wait()

    def remote(s, i):
        return pltpu.make_async_remote_copy(
            send.at[s, pl.ds(i * CAP, CAP)],
            recv.at[s, pl.ds(i * CAP, CAP)],
            send_sem.at[s],
            recv_sem.at[s, i // 16],
            device_id=(other, partner(me, ORDER[i], 1)),
            device_id_type=MESH,
        )

    def gather(s, go):
        lane = lanes((CAP, 128))
        for i, o in enumerate(ORDER):
            first = partner(me, o, 1) * CAP
            for k in range(CAP):
                r = row_s[0, first + k]
                for p in range(4):
                    strips[p, pl.ds(i * CAP + k, 1), :] = state[p, pl.ds(r, 1), :]
            at = pl.ds(i * CAP, CAP)
            a, b, c, d = (strips[p, at, :] for p in range(4))
            b, c = roll(b, 96), roll(c, 64)
            send[s, at, 0:128] = jnp.where(lane < D, a, b)
            send[s, at, 128:256] = jnp.where(lane < 64, b, c)
            send[s, at, 256:384] = jnp.where(lane < 32, c, roll(d, 32))
            if go:
                remote(s, i).start()

    gather(0, False)

    sub_lane = lanes((1, EDGES))
    offset = jnp.zeros((1, EDGES), jnp.int32)
    for i, o in enumerate(ORDER):
        offset = jnp.where(sub_lane // CAP == i, o, offset)
    z = (me // 16 + 4 - offset // 16) % 4
    y = (me // 4 + 4 - offset // 4 % 4) % 4
    x = (me + 4 - offset % 4) % 4
    source = (z * 16 + y * 4 + x) * CAP + sub_lane % CAP
    order = jnp.where(lax.broadcasted_iota(jnp.int32, (EDGES, EDGES), 0) == source, 1.0, 0.0).astype(BF16)
    listed = jnp.concatenate(
        [slot.astype(F32), mode.astype(F32), lists_v[4].astype(F32), jnp.zeros((13, EDGES), F32)], axis=0
    )
    listed = mm(listed.astype(BF16), order)
    slot = listed[0:1].astype(jnp.int32)
    mode = listed[1:2].astype(jnp.int32)
    weight = jnp.where(slot >= 0, listed[2:3], 0.0)
    modes = rate_v.shape[1]
    table = jnp.concatenate([rate_v[...], coef_v[...], jnp.zeros((5, modes), F32)], axis=0)
    high, rest = split(table)
    middle, low = split(table - high.astype(F32))
    is_mode = jnp.where(lax.broadcasted_iota(jnp.int32, (modes, EDGES), 0) == mode, 1.0, 0.0).astype(BF16)
    pieces = mm(jnp.concatenate([high.astype(F32), middle.astype(F32), low.astype(F32), jnp.zeros((8, modes), F32)], axis=0).astype(BF16), is_mode)
    per_edge = pieces[0:8] + pieces[8:16] + pieces[16:24]
    one = jnp.where(slot >= 0, 1.0, 0.0)
    loss = jnp.where(below, 0.0, weight * per_edge[0:1])
    c_re = jnp.where(below, one, weight * per_edge[1:2])
    c_im = jnp.where(below, 0.0, weight * per_edge[2:3])
    of_slot = lax.broadcasted_iota(jnp.int32, (SLOTS, EDGES), 0) == slot
    total = jnp.sum(jnp.where(of_slot, loss, 0.0), axis=1, keepdims=True)
    decay[...] = jnp.broadcast_to(total, (SLOTS, 128))
    columns = jnp.concatenate([c_re, c_im, jnp.zeros((126, EDGES), F32)], axis=0)
    for j in range(EDGES // 128):
        coef_t[j * 128 : (j + 1) * 128, :] = columns[:, j * 128 : (j + 1) * 128].T
    target = jnp.where(slot >= 0, slot * D + mode // 2, -1)

    def mark(g, carry):
        at = pl.multiple_of(g * WIDE, 128)
        row = lax.broadcasted_iota(jnp.int32, (WIDE, EDGES), 0) + at
        hot[pl.ds(at, WIDE), :] = jnp.where(row == target, 1.0, 0.0).astype(BF16)
        return carry

    h = jnp.concatenate([0.5 * (h_v[...] + h_v[...].T), jnp.zeros((D, 128 - D), F32)], axis=1)
    h_hi, h_lo = (jnp.concatenate([w.astype(F32), jnp.zeros((128 - D, 128), F32)], axis=0) for w in split(h))
    factor[:128, :128] = h_hi.astype(BF16)
    factor[128:, :128] = h_hi.astype(BF16)
    factor[:128, 128:] = h_lo.astype(BF16)
    factor[128:, 128:] = jnp.zeros((128, 128), BF16)

    def products(g, carry):
        at = pl.ds(pl.multiple_of(g * WIDE, 8), WIDE)
        for p, q, sign in ((0, 1, -1), (1, 0, 1), (2, 3, 1), (3, 2, -1)):
            r = mm(jnp.concatenate(split(state[q, at, :]), axis=1), factor[...])
            r = r[:, :128] + r[:, 128:]
            acc[p, at, :] = r if sign > 0 else -r
        return carry

    def whole(s, first, count):
        at = pl.ds(first, count)
        return pltpu.make_async_remote_copy(
            send.at[s, at], recv.at[s, at], send_sem.at[s], recv_sem.at[s, first // 128],
            device_id=(other, me), device_id_type=MESH,
        )

    def receive(s, chunk):
        whole(s, chunk * 128, 128).wait_recv()
        lane = lanes((2 * CAP, 128))

        def unpack(i, carry):
            row = pl.multiple_of(i * 2 * CAP, 2 * CAP)
            at = pl.ds(chunk * 128 + row, 2 * CAP)
            a, t1, t2 = (recv[s, at, q * 128 : (q + 1) * 128] for q in range(3))
            b = jnp.where(lane < 32, roll(a, 32), roll(t1, 32))
            c = jnp.where(lane < 64, roll(t1, 64), roll(t2, 64))
            d = roll(t2, 96)
            c_re, c_im = coef_t[at, 0:1], coef_t[at, 1:2]
            v = jnp.concatenate(
                [c_im * a + c_re * b, c_im * b - c_re * a, c_im * c - c_re * d, c_im * d + c_re * c], axis=1
            )
            high, low = split(v)
            v_both[pl.ds(chunk * 256 + row, 2 * CAP), :] = high
            v_both[pl.ds(chunk * 256 + 128 + row, 2 * CAP), :] = low
            return carry

        lax.fori_loop(0, 8, unpack, 0, unroll=8)

    def scattered(base, first, last):
        marks = []
        for chunk in range(first, last):
            marks += [hot[pl.ds(base, WIDE), chunk * 128 : (chunk + 1) * 128]] * 2
        return mm(jnp.concatenate(marks, axis=1), v_both[first * 256 : last * 256, :])

    def scatter(g, carry):
        base = pl.multiple_of(g * WIDE, 128)
        added = scattered(base, 0, EARLY)
        for p in range(4):
            acc[p, pl.ds(base, WIDE), :] += added[:, p * 128 : (p + 1) * 128]
        return carry

    def combine(g, carry, last):
        base = pl.multiple_of(g * WIDE, 128)
        added = scattered(base, EARLY, CHUNKS)
        results = []
        for j in range(GROUP):
            at = pl.ds(pl.multiple_of(base + j * D, 8), D)
            a_re, a_im, b_re, b_im = (
                acc[p, at, :] + added[j * D : (j + 1) * D, p * 128 : (p + 1) * 128] for p in range(4)
            )
            rate = decay[pl.ds(g * GROUP + j, 1), :]
            x_re, x_im = state[0, at, :], state[1, at, :]
            s_re = a_re + turn(b_re)[:D] - rate * x_re
            s_im = a_im + turn(b_im)[:D] - rate * x_im
            if last:
                results.append((s_re, s_im))
            else:
                y_re, y_im = state[2, at, :], state[3, at, :]
                state[0, at, :] = x_re + HALF_STEP * s_re
                state[1, at, :] = x_im + HALF_STEP * s_im
                state[2, at, :] = y_re + HALF_STEP * (turn(a_re)[:D] + b_re - rate * y_re)
                state[3, at, :] = y_im + HALF_STEP * (turn(a_im)[:D] + b_im - rate * y_im)
        if last:
            lane = lanes((D, 128))
            at = pl.ds(base, WIDE)
            for p in range(2):
                s0, s1, s2, s3 = (r[p] for r in results)
                s1, s2 = roll(s1, 96), roll(s2, 64)
                out_v[p, :, pl.ds(base, 128)] = jnp.where(lane < D, s0, s1)
                out_v[p, :, pl.ds(pl.multiple_of(base + 128, 128), 128)] = jnp.where(lane < 64, s1, s2)
                out_v[p, :, pl.ds(pl.multiple_of(base + 256, 128), 128)] = jnp.where(lane < 32, s2, roll(s3, 32))
        return carry

    for s in range(2):
        if s:
            gather(s, True)
        else:
            pl.semaphore_wait(barrier, SUBS)
            for i in range(SUBS):
                remote(s, i).start()
            lax.fori_loop(0, GROUPS, mark, 0)
        lax.fori_loop(0, GROUPS, products, 0, unroll=2)
        for chunk in range(CHUNKS):
            receive(s, chunk)
            if chunk == EARLY - 1:
                lax.fori_loop(0, GROUPS, scatter, 0, unroll=2)
        lax.fori_loop(0, GROUPS, functools.partial(combine, last=s == 1), 0, unroll=2)
    for s in range(2):
        whole(s, 0, EDGES).wait_send()


def on_device(ado_field, hamiltonian, decay_rates, bath_coef, counts, child_slot, child_mode, child_occ, parent_slot, parent_mode):
    modes = decay_rates.shape[0]
    scratch = [
        pltpu.VMEM((2, D, ROWS), F32),
        pltpu.VMEM((D, D), F32),
        pltpu.VMEM((1, modes), F32),
        pltpu.VMEM((2, modes), F32),
        pltpu.VMEM((5, 1, EDGES), jnp.int32),
        pltpu.VMEM((1, EDGES), jnp.int32),
        pltpu.SMEM((1, 1), jnp.int32),
        pltpu.SMEM((1, EDGES), jnp.int32),
        pltpu.VMEM((4, ROWS, 128), F32),
        pltpu.VMEM((4, ROWS, 128), F32),
        pltpu.VMEM((ROWS, EDGES), BF16),
        pltpu.VMEM((2 * EDGES, 512), BF16),
        pltpu.VMEM((256, 256), BF16),
        pltpu.VMEM((4, EDGES, 128), F32),
        pltpu.VMEM((2, EDGES, WIDE), F32),
        pltpu.VMEM((2, EDGES, WIDE), F32),
        pltpu.VMEM((EDGES, 128), F32),
        pltpu.VMEM((SLOTS, 128), F32),
        pltpu.SemaphoreType.DMA((GROUPS,)),
        pltpu.SemaphoreType.DMA((9,)),
        pltpu.SemaphoreType.DMA((2,)),
        pltpu.SemaphoreType.DMA((2, CHUNKS)),
    ]
    return pl.pallas_call(
        kernel,
        out_shape=pltpu.VMEM((2, D, ROWS), F32),
        in_specs=[pl.BlockSpec(memory_space=pl.ANY)] * 10,
        out_specs=pl.BlockSpec(memory_space=pltpu.VMEM),
        scratch_shapes=scratch,
        compiler_params=pltpu.CompilerParams(collective_id=0, has_side_effects=True, vmem_limit_bytes=48 << 20),
        cost_estimate=pl.CostEstimate(flops=10**10, bytes_accessed=5 * 10**6, transcendentals=0),
    )(
        *(
            a if a is counts else pltpu.with_memory_space_constraint(a, pltpu.HBM)
            for a in (
                ado_field, hamiltonian, decay_rates.reshape(1, modes), bath_coef, counts,
                child_slot, child_mode, child_occ, parent_slot, parent_mode,
            )
        )
    )


def solution(mesh):
    edges = P("tier", "sub")
    return jax.shard_map(
        on_device,
        mesh=mesh,
        in_specs=(P(None, None, ("tier", "sub")), P(), P(), P(), edges, edges, edges, edges, edges, edges),
        out_specs=P(None, None, ("tier", "sub")),
        check_vma=False,
    )
```

```python
import functools

import jax
import jax.numpy as jnp
from jax import lax
from jax.experimental import pallas as pl
from jax.experimental.pallas import tpu as pltpu
from jax.sharding import PartitionSpec as P

MESH = pl.DeviceIdType.MESH
D = 96
SLOTS = 32
SUBS = 64
CAP = 8
EDGES = SUBS * CAP
ROWS = SLOTS * D
GROUP = 4
WIDE = GROUP * D
GROUPS = SLOTS // GROUP
CHUNKS = EDGES // 128
EARLY = 1
HALF_STEP = 0.1
F32 = jnp.float32
BF16 = jnp.bfloat16


def hops(offset):
    return sum((0, 1, 2, 1)[d] for d in (offset // 16, offset // 4 % 4, offset % 4))


def partner_order():
    seen, groups = set(), []
    for c in range(SUBS):
        v, group = (c // 16, c // 4 % 4, c % 4), []
        for r in range(3):
            for sign in (1, -1):
                u = tuple(sign * v[(r + k) % 3] % 4 for k in range(3))
                if u not in seen:
                    seen.add(u)
                    group.append(u[0] * 16 + u[1] * 4 + u[2])
        if group:
            groups.append(group)
    groups.sort(key=lambda g: -hops(g[0]))
    return [o for g in groups for o in g]


ORDER = partner_order()


def partner(me, offset, sign):
    dz, dy, dx = offset // 16, offset // 4 % 4, offset % 4
    if sign < 0:
        dz, dy, dx = (4 - dz) % 4, (4 - dy) % 4, (4 - dx) % 4
    z, y, x = me // 16, me // 4 % 4, me % 4
    return (z + dz) % 4 * 16 + (y + dy) % 4 * 4 + (x + dx) % 4


def split(value):
    high = value.astype(BF16)
    return high, (value - high.astype(F32)).astype(BF16)


def mm(a, b):
    return jnp.dot(a, b, preferred_element_type=F32)


def roll(value, shift):
    return pltpu.roll(value, shift, 1)


def lanes(shape):
    return lax.broadcasted_iota(jnp.int32, shape, len(shape) - 1)


def turn(value):
    return jnp.concatenate([value, jnp.zeros((128 - D, 128), F32)], axis=0).T


def kernel(
    x_hbm, h_hbm, rate_hbm, coef_hbm, count_hbm, cslot_hbm, cmode_hbm, cocc_hbm, pslot_hbm, pmode_hbm,
    out_v,
    x_v, h_v, rate_v, coef_v, lists_v, row_v, count_s, row_s,
    state, acc, hot, v_both, factor, strips, send, recv, coef_t, decay,
    in_sem, small_sem, send_sem, recv_sem,
):
    tier, me = lax.axis_index("tier"), lax.axis_index("sub")
    other = 1 - tier
    barrier = pltpu.get_barrier_semaphore()
    for o in ORDER:
        pl.semaphore_signal(barrier, 1, device_id=(other, partner(me, o, 1)), device_id_type=MESH)

    smalls = [
        pltpu.make_async_copy(cslot_hbm, lists_v.at[0], small_sem.at[0]),
        pltpu.make_async_copy(pslot_hbm, lists_v.at[1], small_sem.at[1]),
        pltpu.make_async_copy(cmode_hbm, lists_v.at[2], small_sem.at[2]),
        pltpu.make_async_copy(pmode_hbm, lists_v.at[3], small_sem.at[3]),
        pltpu.make_async_copy(cocc_hbm, lists_v.at[4], small_sem.at[4]),
        pltpu.make_async_copy(count_hbm, count_s, small_sem.at[5]),
        pltpu.make_async_copy(h_hbm, h_v, small_sem.at[6]),
        pltpu.make_async_copy(rate_hbm, rate_v, small_sem.at[7]),
        pltpu.make_async_copy(coef_hbm, coef_v, small_sem.at[8]),
    ]
    for copy in smalls:
        copy.start()

    def x_copy(g):
        at = pl.ds(pl.multiple_of(g * WIDE, 128), WIDE)
        return pltpu.make_async_copy(x_hbm.at[:, :, at], x_v.at[:, :, at], in_sem.at[g])

    for g in range(GROUPS):
        x_copy(g).start()
    for copy in smalls:
        copy.wait()

    below = tier == 0
    slot = jnp.where(below, lists_v[1], lists_v[0])
    mode = jnp.where(below, lists_v[3], lists_v[2])
    row_v[...] = jnp.where(slot >= 0, slot * D + mode // 2, 0)
    to_scalars = pltpu.make_async_copy(row_v, row_s, small_sem.at[0])
    to_scalars.start()

    count = count_s[0, 0]

    def load(g, carry):
        x_copy(g).wait()
        at = pl.ds(pl.multiple_of(g * WIDE, 128), WIDE)
        live = lanes((D, WIDE)) // D + g * GROUP < count
        lane = lanes((D, 128))
        for p in range(2):
            x = jnp.where(live, x_v[p, :, at], 0.0)
            t0, t1, t2 = x[:, :128], x[:, 128:256], x[:, 256:]
            parts = (
                t0,
                jnp.where(lane < 32, roll(t0, 32), roll(t1, 32)),
                jnp.where(lane < 64, roll(t1, 64), roll(t2, 64)),
                roll(t2, 96),
            )
            for j, part in enumerate(parts):
                state[p, pl.ds(pl.multiple_of(g * WIDE + j * D, 8), D), :] = part
            for j, part in enumerate((t0, t1, t2)):
                state[2 + p, pl.ds(pl.multiple_of(g * WIDE + j * 128, 8), 128), :] = turn(part)
        return carry

    lax.fori_loop(0, GROUPS, load, 0)
    to_scalars.wait()

    def remote(s, i):
        return pltpu.make_async_remote_copy(
            send.at[s, pl.ds(i * CAP, CAP)],
            recv.at[s, pl.ds(i * CAP, CAP)],
            send_sem.at[s],
            recv_sem.at[s, i // 16],
            device_id=(other, partner(me, ORDER[i], 1)),
            device_id_type=MESH,
        )

    def gather(s, go):
        lane = lanes((CAP, 128))
        for i, o in enumerate(ORDER):
            first = partner(me, o, 1) * CAP
            for k in range(CAP):
                r = row_s[0, first + k]
                for p in range(4):
                    strips[p, pl.ds(i * CAP + k, 1), :] = state[p, pl.ds(r, 1), :]
            at = pl.ds(i * CAP, CAP)
            a, b, c, d = (strips[p, at, :] for p in range(4))
            b, c = roll(b, 96), roll(c, 64)
            send[s, at, 0:128] = jnp.where(lane < D, a, b)
            send[s, at, 128:256] = jnp.where(lane < 64, b, c)
            send[s, at, 256:384] = jnp.where(lane < 32, c, roll(d, 32))
            if go:
                remote(s, i).start()

    gather(0, False)

    sub_lane = lanes((1, EDGES))
    offset = jnp.zeros((1, EDGES), jnp.int32)
    for i, o in enumerate(ORDER):
        offset = jnp.where(sub_lane // CAP == i, o, offset)
    z = (me // 16 + 4 - offset // 16) % 4
    y = (me // 4 + 4 - offset // 4 % 4) % 4
    x = (me + 4 - offset % 4) % 4
    source = (z * 16 + y * 4 + x) * CAP + sub_lane % CAP
    order = jnp.where(lax.broadcasted_iota(jnp.int32, (EDGES, EDGES), 0) == source, 1.0, 0.0).astype(BF16)
    listed = jnp.concatenate(
        [slot.astype(F32), mode.astype(F32), lists_v[4].astype(F32), jnp.zeros((13, EDGES), F32)], axis=0
    )
    listed = mm(listed.astype(BF16), order)
    slot = listed[0:1].astype(jnp.int32)
    mode = listed[1:2].astype(jnp.int32)
    weight = jnp.where(slot >= 0, listed[2:3], 0.0)
    modes = rate_v.shape[1]
    table = jnp.concatenate([rate_v[...], coef_v[...], jnp.zeros((5, modes), F32)], axis=0)
    high, rest = split(table)
    middle, low = split(table - high.astype(F32))
    is_mode = jnp.where(lax.broadcasted_iota(jnp.int32, (modes, EDGES), 0) == mode, 1.0, 0.0).astype(BF16)
    pieces = mm(jnp.concatenate([high.astype(F32), middle.astype(F32), low.astype(F32), jnp.zeros((8, modes), F32)], axis=0).astype(BF16), is_mode)
    per_edge = pieces[0:8] + pieces[8:16] + pieces[16:24]
    one = jnp.where(slot >= 0, 1.0, 0.0)
    loss = jnp.where(below, 0.0, weight * per_edge[0:1])
    c_re = jnp.where(below, one, weight * per_edge[1:2])
    c_im = jnp.where(below, 0.0, weight * per_edge[2:3])
    of_slot = lax.broadcasted_iota(jnp.int32, (SLOTS, EDGES), 0) == slot
    total = jnp.sum(jnp.where(of_slot, loss, 0.0), axis=1, keepdims=True)
    decay[...] = jnp.broadcast_to(total, (SLOTS, 128))
    columns = jnp.concatenate([c_re, c_im, jnp.zeros((126, EDGES), F32)], axis=0)
    for j in range(EDGES // 128):
        coef_t[j * 128 : (j + 1) * 128, :] = columns[:, j * 128 : (j + 1) * 128].T
    target = jnp.where(slot >= 0, slot * D + mode // 2, -1)

    def mark(g, carry):
        at = pl.multiple_of(g * WIDE, 128)
        row = lax.broadcasted_iota(jnp.int32, (WIDE, EDGES), 0) + at
        hot[pl.ds(at, WIDE), :] = jnp.where(row == target, 1.0, 0.0).astype(BF16)
        return carry

    h = jnp.concatenate([0.5 * (h_v[...] + h_v[...].T), jnp.zeros((D, 128 - D), F32)], axis=1)
    h_hi, h_lo = (jnp.concatenate([w.astype(F32), jnp.zeros((128 - D, 128), F32)], axis=0) for w in split(h))
    factor[:128, :128] = h_hi.astype(BF16)
    factor[128:, :128] = h_hi.astype(BF16)
    factor[:128, 128:] = h_lo.astype(BF16)
    factor[128:, 128:] = jnp.zeros((128, 128), BF16)

    def products(g, carry):
        at = pl.ds(pl.multiple_of(g * WIDE, 8), WIDE)
        for p, q, sign in ((0, 1, -1), (1, 0, 1), (2, 3, 1), (3, 2, -1)):
            r = mm(jnp.concatenate(split(state[q, at, :]), axis=1), factor[...])
            r = r[:, :128] + r[:, 128:]
            acc[p, at, :] = r if sign > 0 else -r
        return carry

    def whole(s, first, count):
        at = pl.ds(first, count)
        return pltpu.make_async_remote_copy(
            send.at[s, at], recv.at[s, at], send_sem.at[s], recv_sem.at[s, first // 128],
            device_id=(other, me), device_id_type=MESH,
        )

    def receive(s, chunk):
        whole(s, chunk * 128, 128).wait_recv()
        lane = lanes((2 * CAP, 128))

        def unpack(i, carry):
            row = pl.multiple_of(i * 2 * CAP, 2 * CAP)
            at = pl.ds(chunk * 128 + row, 2 * CAP)
            a, t1, t2 = (recv[s, at, q * 128 : (q + 1) * 128] for q in range(3))
            b = jnp.where(lane < 32, roll(a, 32), roll(t1, 32))
            c = jnp.where(lane < 64, roll(t1, 64), roll(t2, 64))
            d = roll(t2, 96)
            c_re, c_im = coef_t[at, 0:1], coef_t[at, 1:2]
            v = jnp.concatenate(
                [c_im * a + c_re * b, c_im * b - c_re * a, c_im * c - c_re * d, c_im * d + c_re * c], axis=1
            )
            high, low = split(v)
            v_both[pl.ds(chunk * 256 + row, 2 * CAP), :] = high
            v_both[pl.ds(chunk * 256 + 128 + row, 2 * CAP), :] = low
            return carry

        lax.fori_loop(0, 8, unpack, 0, unroll=8)

    def scattered(base, first, last):
        marks = []
        for chunk in range(first, last):
            marks += [hot[pl.ds(base, WIDE), chunk * 128 : (chunk + 1) * 128]] * 2
        return mm(jnp.concatenate(marks, axis=1), v_both[first * 256 : last * 256, :])

    def scatter(g, carry):
        base = pl.multiple_of(g * WIDE, 128)
        added = scattered(base, 0, EARLY)
        for p in range(4):
            acc[p, pl.ds(base, WIDE), :] += added[:, p * 128 : (p + 1) * 128]
        return carry

    def combine(g, carry, last):
        base = pl.multiple_of(g * WIDE, 128)
        added = scattered(base, EARLY, CHUNKS)
        results = []
        for j in range(GROUP):
            at = pl.ds(pl.multiple_of(base + j * D, 8), D)
            a_re, a_im, b_re, b_im = (
                acc[p, at, :] + added[j * D : (j + 1) * D, p * 128 : (p + 1) * 128] for p in range(4)
            )
            rate = decay[pl.ds(g * GROUP + j, 1), :]
            x_re, x_im = state[0, at, :], state[1, at, :]
            s_re = a_re + turn(b_re)[:D] - rate * x_re
            s_im = a_im + turn(b_im)[:D] - rate * x_im
            if last:
                results.append((s_re, s_im))
            else:
                y_re, y_im = state[2, at, :], state[3, at, :]
                state[0, at, :] = x_re + HALF_STEP * s_re
                state[1, at, :] = x_im + HALF_STEP * s_im
                state[2, at, :] = y_re + HALF_STEP * (turn(a_re)[:D] + b_re - rate * y_re)
                state[3, at, :] = y_im + HALF_STEP * (turn(a_im)[:D] + b_im - rate * y_im)
        if last:
            lane = lanes((D, 128))
            at = pl.ds(base, WIDE)
            for p in range(2):
                s0, s1, s2, s3 = (r[p] for r in results)
                s1, s2 = roll(s1, 96), roll(s2, 64)
                out_v[p, :, pl.ds(base, 128)] = jnp.where(lane < D, s0, s1)
                out_v[p, :, pl.ds(pl.multiple_of(base + 128, 128), 128)] = jnp.where(lane < 64, s1, s2)
                out_v[p, :, pl.ds(pl.multiple_of(base + 256, 128), 128)] = jnp.where(lane < 32, s2, roll(s3, 32))
        return carry

    for s in range(2):
        if s:
            gather(s, True)
        else:
            pl.semaphore_wait(barrier, SUBS)
            for i in range(SUBS):
                remote(s, i).start()
            lax.fori_loop(0, GROUPS, mark, 0)
        lax.fori_loop(0, GROUPS, products, 0, unroll=2)
        for chunk in range(CHUNKS):
            receive(s, chunk)
            if chunk == EARLY - 1:
                lax.fori_loop(0, GROUPS, scatter, 0, unroll=2)
        lax.fori_loop(0, GROUPS, functools.partial(combine, last=s == 1), 0, unroll=8)
    for s in range(2):
        whole(s, 0, EDGES).wait_send()


def on_device(ado_field, hamiltonian, decay_rates, bath_coef, counts, child_slot, child_mode, child_occ, parent_slot, parent_mode):
    modes = decay_rates.shape[0]
    scratch = [
        pltpu.VMEM((2, D, ROWS), F32),
        pltpu.VMEM((D, D), F32),
        pltpu.VMEM((1, modes), F32),
        pltpu.VMEM((2, modes), F32),
        pltpu.VMEM((5, 1, EDGES), jnp.int32),
        pltpu.VMEM((1, EDGES), jnp.int32),
        pltpu.SMEM((1, 1), jnp.int32),
        pltpu.SMEM((1, EDGES), jnp.int32),
        pltpu.VMEM((4, ROWS, 128), F32),
        pltpu.VMEM((4, ROWS, 128), F32),
        pltpu.VMEM((ROWS, EDGES), BF16),
        pltpu.VMEM((2 * EDGES, 512), BF16),
        pltpu.VMEM((256, 256), BF16),
        pltpu.VMEM((4, EDGES, 128), F32),
        pltpu.VMEM((2, EDGES, WIDE), F32),
        pltpu.VMEM((2, EDGES, WIDE), F32),
        pltpu.VMEM((EDGES, 128), F32),
        pltpu.VMEM((SLOTS, 128), F32),
        pltpu.SemaphoreType.DMA((GROUPS,)),
        pltpu.SemaphoreType.DMA((9,)),
        pltpu.SemaphoreType.DMA((2,)),
        pltpu.SemaphoreType.DMA((2, CHUNKS)),
    ]
    return pl.pallas_call(
        kernel,
        out_shape=pltpu.VMEM((2, D, ROWS), F32),
        in_specs=[pl.BlockSpec(memory_space=pl.ANY)] * 10,
        out_specs=pl.BlockSpec(memory_space=pltpu.VMEM),
        scratch_shapes=scratch,
        compiler_params=pltpu.CompilerParams(collective_id=0, has_side_effects=True, vmem_limit_bytes=48 << 20),
        cost_estimate=pl.CostEstimate(flops=10**10, bytes_accessed=5 * 10**6, transcendentals=0),
    )(
        *(
            a if a is counts else pltpu.with_memory_space_constraint(a, pltpu.HBM)
            for a in (
                ado_field, hamiltonian, decay_rates.reshape(1, modes), bath_coef, counts,
                child_slot, child_mode, child_occ, parent_slot, parent_mode,
            )
        )
    )


def solution(mesh):
    edges = P("tier", "sub")
    return jax.shard_map(
        on_device,
        mesh=mesh,
        in_specs=(P(None, None, ("tier", "sub")), P(), P(), P(), edges, edges, edges, edges, edges, edges),
        out_specs=P(None, None, ("tier", "sub")),
        check_vma=False,
    )
```
